32 devices in a mesh: groups: 2 (over y), replica: 4 (over x, core), tensor: 4 (over z).
Axes of the slice: x: 2, y: 2, z: 4, core: 2. Of those that a mesh axis runs over, the one named last changes fastest.
Arguments:
- tokens: bfloat16 [8, 768, 4096], P(('groups', 'replica'), None, 'tensor'), parts along dimension 0, may hold values from -16 to 16
- lengths: int32 [8], P(('groups', 'replica')), parts along dimension 0, may hold values from 1 to 768, 1536 in all
- block_adapter_index: int32 [8], P(('groups', 'replica')), parts along dimension 0, may hold values from 0 to 7
- cache_page_index: int32 [8, 12], P(('groups', 'replica')), parts along dimension 0, may hold values from 0 to 11, each once within a row
- query_matrix: bfloat16 [4096, 2048], P(None, 'tensor'), may hold values from -0.09375 to 0.09375
- key_matrix: bfloat16 [4096, 512], P(None, 'tensor'), may hold values from -0.09375 to 0.09375
- value_matrix: bfloat16 [4096, 512], P(None, 'tensor'), may hold values from -0.09375 to 0.09375
- down_factors: bfloat16 [8, 4096, 128], P('replica', 'tensor'), may hold values from -0.09375 to 0.09375
- query_up_factors: bfloat16 [8, 64, 2048], P('replica', None, 'tensor'), may hold values from -0.75 to 0.75
- value_up_factors: bfloat16 [8, 64, 512], P('replica', None, 'tensor'), may hold values from -0.75 to 0.75
Outputs:
- attended: bfloat16 [8, 768, 2048], P(('groups', 'replica'), None, 'tensor'), parts along dimension 0
- kv_pages: bfloat16 [8, 12, 2, 64, 512], P(('groups', 'replica'), None, None, None, 'tensor'), parts along dimension 0
The draws below stay inside these ranges and needn't reach their ends.
There are 2 independent parts, one for each index of `groups`. The reference program is written for one: setup_inputs(seed, part) draws one part's arguments, and reference() takes and returns one part's arrays. A program takes and returns all parts, laid end to end along the dimension named above; an argument that names none is the same for every part. Nothing has to cross between parts.
Inputs may be any that keep to these rules, and one draw needn't show every extreme that they name: The lengths of one part sum to 1536, and some block is 768 long. `cache_page_index`: each row is a permutation of the block's pages.
All inputs are finite; a program needn't handle non-finite values.
Results may differ from the reference program's by a relative error of at most 0.008.
The reference program's roundings to bfloat16 on the way count: a program that leaves them out, or rounds other values in their place, can miss the bound.
Values may be sent and summed in bfloat16 or wider, within the bound.
A program may use at most 64 MiB of HBM per device.

```python
import math
import jax
import jax.numpy as jnp
import numpy as np
from jax import lax

MODEL_WIDTH = 4096
HEAD_SIZE = 128
QUERY_HEADS = 16
KEY_VALUE_HEADS = 4
ADAPTER_RANK = 64
ADAPTER_COUNT = 8
BLOCK = 768
PAGE = 64
PAGES = 12
REPLICAS = 4


def draw_tokens(key, part):
    key = jax.random.fold_in(key, 11)
    first_key = jax.random.fold_in(key, 0)
    values = jnp.clip(jax.random.normal(first_key, (REPLICAS, BLOCK, MODEL_WIDTH), jnp.float32), -4.0, 4.0)
    return values.astype(jnp.bfloat16)


def with_ends(values, key, smallest, high):
    spot = [jax.random.randint(jax.random.fold_in(key, axis), (), 0, length) for axis, length in enumerate(values.shape)]
    widest = values.shape.index(max(values.shape))
    next_to = spot[:widest] + [(spot[widest] + 1) % values.shape[widest]] + spot[widest + 1:]
    return values.at[tuple(spot)].set(smallest).at[tuple(next_to)].set(high)


def steps_of(own_key, shape, pieces, smallest, top_value):
    loudness = 1.0
    for axis_at, blocks in pieces:
        steps = jax.random.uniform(jax.random.fold_in(jax.random.fold_in(own_key, 6), axis_at), (blocks,), jnp.float32, smallest / len(pieces), top_value / len(pieces))
        loudness = loudness * jnp.repeat(jnp.exp(steps), shape[axis_at] // blocks).reshape((-1,) + (1,) * (len(shape) - 1 - axis_at))
    return loudness


def split_up(number_of, total, reach, lean):
    portions = [(1 << 20) // math.isqrt(grade ** lean) + 1 for grade in range(2, number_of + 1)]
    surplus, given = total - reach - (number_of - 1), [1] * (number_of - 1)
    while surplus > 0:
        candidates = [i for i in range(number_of - 1) if given[i] < reach]
        pool, remaining = sum([portions[i] for i in candidates]), surplus
        for i in candidates:
            addition = min(reach - given[i], max(1, remaining * portions[i] // pool), surplus)
            given[i] = given[i] + addition
            surplus = surplus - addition
    return np.array([reach] + given)


def ragged(key, number_of, total, bound, lean):
    if number_of == 2:
        one = jax.random.randint(key, (), max(1, total - bound), min(bound, total - 1) + 1)
        return jnp.stack([one, total - one])
    sizes = jnp.asarray(split_up(number_of, total, bound, lean), jnp.int32)
    couples = (number_of - 1) // 2
    source_of, taker = sizes[1:1 + 2 * couples:2], sizes[2:2 + 2 * couples:2]
    slack = jnp.minimum(source_of - 1, bound - taker)
    passed = jax.random.randint(jax.random.fold_in(key, 1), (couples,), 0, 1 << 20) % (slack + 1)
    sizes = sizes.at[1:1 + 2 * couples:2].set(source_of - passed).at[2:2 + 2 * couples:2].set(taker + passed)
    return sizes[jax.random.permutation(jax.random.fold_in(key, 2), number_of)]


def scatter_about(key, shape, scale, bound, cuts=(), kind=jnp.bfloat16):
    gain = steps_of(key, shape, cuts, -0.22, 0.18) if cuts else 1.0
    array = jax.random.normal(key, shape, jnp.float32) * scale * gain
    return jnp.minimum(jnp.maximum(array, -bound), bound).astype(kind)


def setup_inputs(seed: int = 0, part: int = 0) -> dict:
    arg_keys = jax.random.split(jax.random.key(seed), 11)
    part_keys = jax.random.split(jax.random.fold_in(arg_keys[10], part), 11)
    tokens = draw_tokens(jax.random.fold_in(jax.random.fold_in(arg_keys[10], part), 71), part)
    lengths = ragged(part_keys[1], REPLICAS, REPLICAS * BLOCK // 2, BLOCK, 2).astype(jnp.int32)
    block_adapter_index = with_ends(jax.random.randint(part_keys[2], (REPLICAS,), 0, ADAPTER_COUNT), jax.random.fold_in(part_keys[2], 1), 0, ADAPTER_COUNT - 1).astype(jnp.int32)
    cache_page_index = jax.vmap(lambda own: jax.random.permutation(own, PAGES))(jax.random.split(part_keys[3], REPLICAS)).reshape((REPLICAS, PAGES)).astype(jnp.int32)
    query_matrix = scatter_about(arg_keys[4], (MODEL_WIDTH, QUERY_HEADS * HEAD_SIZE), MODEL_WIDTH ** -0.5, 0.09375, ((1, 4),))
    key_matrix = scatter_about(arg_keys[5], (MODEL_WIDTH, KEY_VALUE_HEADS * HEAD_SIZE), MODEL_WIDTH ** -0.5, 0.09375, ((1, 4),))
    value_matrix = scatter_about(arg_keys[6], (MODEL_WIDTH, KEY_VALUE_HEADS * HEAD_SIZE), MODEL_WIDTH ** -0.5, 0.09375, ((1, 4),))
    down_factors = scatter_about(arg_keys[7], (ADAPTER_COUNT, MODEL_WIDTH, 2 * ADAPTER_RANK), MODEL_WIDTH ** -0.5, 0.09375, ((0, 4), (1, 4)))
    query_up_factors = scatter_about(arg_keys[8], (ADAPTER_COUNT, ADAPTER_RANK, QUERY_HEADS * HEAD_SIZE), ADAPTER_RANK ** -0.5, 0.75, ((0, 4), (2, 4)))
    value_up_factors = scatter_about(arg_keys[9], (ADAPTER_COUNT, ADAPTER_RANK, KEY_VALUE_HEADS * HEAD_SIZE), ADAPTER_RANK ** -0.5, 0.75, ((0, 4), (2, 4)))
    return dict(tokens=tokens, lengths=lengths, block_adapter_index=block_adapter_index, cache_page_index=cache_page_index, query_matrix=query_matrix, key_matrix=key_matrix, value_matrix=value_matrix, down_factors=down_factors, query_up_factors=query_up_factors, value_up_factors=value_up_factors)


def rope_tables(length, width):
    half_width = width // 2
    exponent = 2.0 * jnp.arange(half_width, dtype=jnp.float32) / width
    frequency = jnp.exp(-jnp.log(500000.0) * exponent)
    angles = jnp.arange(length, dtype=jnp.float32)[:, None] * frequency[None, :]
    return jnp.cos(angles), jnp.sin(angles)


def rotate(values, cosine, sine):
    half_width = values.shape[-1] // 2
    first = values[..., :half_width]
    second = values[..., half_width:]
    cos_rows = cosine[:, None, :]
    sin_rows = sine[:, None, :]
    return jnp.concatenate([first * cos_rows - second * sin_rows, second * cos_rows + first * sin_rows], axis=-1)


def single_block(input_rows, query_matrix, key_matrix, value_matrix, down_factors, query_up_factors, value_up_factors):
    rows_of_block, length, chosen_adapter, page_order = input_rows
    row_count = rows_of_block.shape[0]
    q_heads = query_matrix.shape[1] // HEAD_SIZE
    kv_heads = key_matrix.shape[1] // HEAD_SIZE
    group_size = q_heads // kv_heads
    rank_total = query_up_factors.shape[1]
    query_plain = jnp.dot(rows_of_block, query_matrix, preferred_element_type=jnp.float32)
    k_base = jnp.dot(rows_of_block, key_matrix, preferred_element_type=jnp.float32)
    value_plain = jnp.dot(rows_of_block, value_matrix, preferred_element_type=jnp.float32)
    down_projected = jnp.dot(rows_of_block, down_factors[chosen_adapter], preferred_element_type=jnp.float32).astype(jnp.bfloat16)
    query_adapted = query_plain + jnp.dot(down_projected[:, :rank_total], query_up_factors[chosen_adapter], preferred_element_type=jnp.float32)
    value_adapted = value_plain + jnp.dot(down_projected[:, rank_total:], value_up_factors[chosen_adapter], preferred_element_type=jnp.float32)
    cosine, sine = rope_tables(row_count, HEAD_SIZE)
    q_rot = rotate(query_adapted.reshape(row_count, q_heads, HEAD_SIZE), cosine, sine)
    k_rot = rotate(k_base.reshape(row_count, kv_heads, HEAD_SIZE), cosine, sine)
    positions = jnp.arange(row_count, dtype=jnp.int32)
    live = positions < length
    query = q_rot.astype(jnp.bfloat16)
    key_rows = jnp.where(live[:, None, None], k_rot, 0.0).astype(jnp.bfloat16)
    value_rows = jnp.where(live[:, None], value_adapted, 0.0).astype(jnp.bfloat16).reshape(row_count, kv_heads, HEAD_SIZE)
    grouped = query.reshape(row_count, kv_heads, group_size, HEAD_SIZE).astype(jnp.float32)
    scores = jnp.einsum('tkgd,skd->kgts', grouped, key_rows.astype(jnp.float32)) * (HEAD_SIZE ** -0.5)
    causal = positions[None, :] <= positions[:, None]
    scores = jnp.where(causal, scores, -jnp.inf)
    peak = jnp.max(scores, axis=-1, keepdims=True)
    weights = jnp.exp(scores - peak)
    probs = (weights / jnp.sum(weights, axis=-1, keepdims=True)).astype(jnp.bfloat16)
    mixed = jnp.einsum('kgts,skd->tkgd', probs.astype(jnp.float32), value_rows.astype(jnp.float32))
    attended = jnp.where(live[:, None], mixed.reshape(row_count, q_heads * HEAD_SIZE), 0.0).astype(jnp.bfloat16)
    keys_paged = key_rows.reshape(row_count // PAGE, PAGE, kv_heads * HEAD_SIZE)
    values_paged = value_rows.reshape(row_count // PAGE, PAGE, kv_heads * HEAD_SIZE)
    stacked = jnp.stack([keys_paged, values_paged], axis=1)
    pages = jnp.zeros_like(stacked).at[page_order].set(stacked)
    return attended, pages


def reference(tokens, lengths, block_adapter_index, cache_page_index, query_matrix, key_matrix, value_matrix, down_factors, query_up_factors, value_up_factors):
    def apply_block(input_rows):
        return single_block(input_rows, query_matrix, key_matrix, value_matrix, down_factors, query_up_factors, value_up_factors)

    attended, kv_pages = lax.map(apply_block, (tokens, lengths, block_adapter_index, cache_page_index))
    return attended, kv_pages
```

```python
import functools

import jax
import jax.numpy as jnp
import numpy as np
from jax import lax
from jax.experimental import pallas as pl
from jax.experimental.pallas import tpu as pltpu
from jax.sharding import PartitionSpec as P

HEAD_SIZE = 128
PAGE = 64
CHUNKS = 4


def rope_tables(length, width):
    half = width // 2
    exponent = np.float32(2.0) * np.arange(half, dtype=np.float32) / np.float32(width)
    frequency = np.exp(-np.log(np.float32(500000.0)) * exponent).astype(np.float32)
    angles = np.arange(length, dtype=np.float32)[:, None] * frequency[None, :]
    cosine, sine = np.cos(angles), np.sin(angles)
    return (
        np.concatenate([cosine, cosine], axis=1).astype(np.float32),
        np.concatenate([-sine, sine], axis=1).astype(np.float32),
    )


def project_kernel(
    n_t, n_r, x_ref, aid_ref, live_ref, cos_ref, sin_ref, wq_ref, wk_ref, wv_ref, dn_ref, uq_ref, uv_ref,
    out_ref,
    xg, acc, dg, ugq, ugv, part, pr, sh, shg,
    zs, zr, asend, arecv, rs_s, rs_r, ag_s, ag_r,
):
    me = lax.axis_index("tensor")
    rep = lax.axis_index("replica")
    chip, core = rep // 2, rep % 2
    n_x = n_r // 2
    mate = chip * 2 + 1 - core
    T, F = x_ref.shape
    R = T // CHUNKS
    S = T // n_t
    per = dn_ref.shape[0]
    rank = uq_ref.shape[1]
    qw, kw = wq_ref.shape[1], wk_ref.shape[1]

    def tensor_peer(i):
        return lax.rem(me + i, n_t)

    def same_core(i):
        return lax.rem(chip + i, n_x) * 2 + core

    barrier = pltpu.get_barrier_semaphore()
    for i in range(1, n_t):
        pl.semaphore_signal(barrier, inc=1, device_id={"tensor": tensor_peer(i)})
    for i in range(1, n_x):
        pl.semaphore_signal(barrier, inc=1, device_id={"replica": same_core(i)})
    pl.semaphore_signal(barrier, inc=1, device_id={"replica": mate})
    pl.semaphore_wait(barrier, n_t - 1 + n_x - 1 + 1)

    def rows_of(c):
        return pl.ds(pl.multiple_of(c * R, R), R)

    def item(side, d, c):
        sgn = 1 - 2 * side
        ref = xg.at[me - sgn * d, rows_of(c)]
        return pltpu.make_async_remote_copy(
            src_ref=ref, dst_ref=ref, send_sem=zs.at[side, d, c], recv_sem=zr.at[side, d, c],
            device_id={"tensor": me + sgn})

    def arrival(side, d, c):
        sgn = 1 - 2 * side
        ref = xg.at[me - sgn * d, rows_of(c)]
        return pltpu.make_async_remote_copy(
            src_ref=ref, dst_ref=ref, send_sem=zs.at[side, d - 1, c], recv_sem=zr.at[side, d - 1, c],
            device_id={"tensor": me})

    def inside(t):
        return (t >= 0) & (t < n_t)

    def send_own(c, carry):
        xg[me, rows_of(c)] = x_ref[rows_of(c)]
        for side in range(2):
            @pl.when(inside(me + 1 - 2 * side))
            def _():
                item(side, 0, c).start()
        return carry

    lax.fori_loop(0, CHUNKS, send_own, 0)

    pools = ((dn_ref, dg), (uq_ref, ugq), (uv_ref, ugv))

    def pool_copy(k, slot, i, j, to, own):
        src = pools[k][0] if own else pools[k][1].at[slot]
        return pltpu.make_async_remote_copy(
            src_ref=src, dst_ref=pools[k][1].at[slot], send_sem=asend.at[k, i, j],
            recv_sem=arecv.at[k, i, j], device_id={"replica": to})

    for k in range(3):
        for i in range(1, n_x):
            pool_copy(k, rep, i, 0, same_core(i), True).start()
        pool_copy(k, rep, 0, 1, mate, True).start()
        pools[k][1][rep] = pools[k][0][...]

    def mac(src, c, first=False):
        rows = rows_of(c)
        x = xg[src, rows]
        feat = pl.ds(pl.multiple_of(src * F, F), F)
        lo = 0
        for w_ref in (wq_ref, wk_ref, wv_ref):
            width = w_ref.shape[1]
            term = jnp.dot(x, w_ref[feat, :], preferred_element_type=jnp.float32)
            if first:
                acc[rows, lo:lo + width] = term
            else:
                acc[rows, lo:lo + width] += term
            lo += width

    def own_mac(c, carry):
        mac(me, c, True)
        return carry

    lax.fori_loop(0, CHUNKS, own_mac, 0)

    for i in range(1, n_x):
        slot = lax.rem(chip + n_x - i, n_x) * 2 + core
        for k in range(3):
            pool_copy(k, slot, i, 0, mate, False).wait_recv()
            pool_copy(k, slot, i, 1, mate, False).start()
    for i in range(n_x):
        slot = lax.rem(chip + n_x - i, n_x) * 2 + 1 - core
        for k in range(3):
            pool_copy(k, slot, i, 1, mate, False).wait_recv()

    part[...] = jnp.zeros_like(part)

    def down(a, carry):
        term = jnp.dot(x_ref[...], dg[a // per, a % per], preferred_element_type=jnp.float32)
        part[...] += jnp.where(aid_ref[...] == a, term, 0.0)
        return carry

    lax.fori_loop(0, n_r * per, down, 0)

    def rs_copy(t, i):
        return pltpu.make_async_remote_copy(
            src_ref=part.at[pl.ds(pl.multiple_of(t * S, S), S)], dst_ref=pr.at[me],
            send_sem=rs_s.at[i], recv_sem=rs_r.at[i], device_id={"tensor": t})

    def ag_copy(t, i):
        return pltpu.make_async_remote_copy(
            src_ref=sh, dst_ref=shg.at[me], send_sem=ag_s.at[i], recv_sem=ag_r.at[i],
            device_id={"tensor": t})

    for i in range(1, n_t):
        rs_copy(tensor_peer(i), i).start()
    pr[me] = part[pl.ds(pl.multiple_of(me * S, S), S)]

    def phase(first, last):
        def step(k, carry):
            d, c = first + k // CHUNKS, k % CHUNKS

            def one(side, carry):
                sgn = 1 - 2 * side
                src = me - sgn * d

                @pl.when(inside(src))
                def _():
                    arrival(side, d, c).wait_recv()

                    @pl.when(inside(me + sgn))
                    def _():
                        item(side, d, c).start()

                    mac(src, c)

                return carry

            return lax.fori_loop(0, 2, one, carry)

        lax.fori_loop(0, (last - first + 1) * CHUNKS, step, 0)

    phase(1, 1)

    def slot_copy(buf, i, send, recv):
        slot = lax.rem(me + n_t - i, n_t)
        return pltpu.make_async_remote_copy(
            src_ref=buf.at[slot], dst_ref=buf.at[slot], send_sem=send.at[i], recv_sem=recv.at[i],
            device_id={"tensor": me})

    for i in range(1, n_t):
        slot_copy(pr, i, rs_s, rs_r).wait_recv()
    total = pr[0]
    for t in range(1, n_t):
        total = total + pr[t]
    sh[...] = total.astype(jnp.bfloat16)
    for i in range(1, n_t):
        ag_copy(tensor_peer(i), i).start()
    shg[me] = sh[...]

    if n_t > 2:
        phase(2, n_t - 1)

    for i in range(1, n_t):
        slot_copy(shg, i, ag_s, ag_r).wait_recv()

    def finish(t, carry):
        rows = pl.ds(pl.multiple_of(t * S, S), S)
        shrunk = shg[t]
        ids = aid_ref[rows]
        zero = jnp.zeros_like(shrunk)

        def up(a, carry):
            mine = jnp.where(ids == a, shrunk.astype(jnp.float32), 0.0).astype(jnp.bfloat16)
            acc[rows, 0:qw] += jnp.dot(mine[:, :rank], ugq[a // per, a % per], preferred_element_type=jnp.float32)
            acc[rows, qw + kw:] += jnp.dot(mine[:, rank:], ugv[a // per, a % per], preferred_element_type=jnp.float32)
            return carry

        lax.fori_loop(0, n_r * per, up, 0)
        cosine, sine = cos_ref[rows], sin_ref[rows]
        live = live_ref[rows] > 0
        for lo in range(0, qw + 2 * kw, HEAD_SIZE):
            v = acc[rows, lo:lo + HEAD_SIZE]
            if lo < qw + kw:
                v = v * cosine + pltpu.roll(v, HEAD_SIZE // 2, 1) * sine
            if lo >= qw:
                v = jnp.where(live, v, 0.0)
            out_ref[rows, lo:lo + HEAD_SIZE] = v.astype(jnp.bfloat16)
        return carry

    lax.fori_loop(0, n_t, finish, 0)

    def drain(k, carry):
        d, c = k // CHUNKS, k % CHUNKS
        for side in range(2):
            sgn = 1 - 2 * side

            @pl.when(inside(me - sgn * d) & inside(me + sgn))
            def _():
                item(side, d, c).wait_send()
        return carry

    lax.fori_loop(0, (n_t - 1) * CHUNKS, drain, 0)
    for i in range(1, n_t):
        rs_copy(tensor_peer(i), i).wait_send()
        ag_copy(tensor_peer(i), i).wait_send()
    for k in range(3):
        pool_copy(k, rep, 0, 1, mate, True).wait_send()
        for i in range(1, n_x):
            slot = lax.rem(chip + n_x - i, n_x) * 2 + core
            pool_copy(k, rep, i, 0, same_core(i), True).wait_send()
            pool_copy(k, slot, i, 1, mate, False).wait_send()


def attend_kernel(qw, kw, length_ref, page_ref, qkv_ref, out_ref, pages_ref):
    T = qkv_ref.shape[0]
    tile = 256
    group = qw // kw
    length = length_ref[0]
    for p in range(T // PAGE):
        at = page_ref[0, p]
        pages_ref[at, 0] = qkv_ref[p * PAGE:(p + 1) * PAGE, qw:qw + kw]
        pages_ref[at, 1] = qkv_ref[p * PAGE:(p + 1) * PAGE, qw + kw:]
    for i in range(T // tile):
        rows = slice(i * tile, (i + 1) * tile)
        seen = (i + 1) * tile
        t = lax.broadcasted_iota(jnp.int32, (tile, seen), 0) + i * tile
        s = lax.broadcasted_iota(jnp.int32, (tile, seen), 1)
        causal = s <= t
        live = lax.broadcasted_iota(jnp.int32, (tile, HEAD_SIZE), 0) + i * tile < length
        for h in range(qw // HEAD_SIZE):
            g = (h // group) * HEAD_SIZE
            q = qkv_ref[rows, h * HEAD_SIZE:(h + 1) * HEAD_SIZE]
            key = qkv_ref[0:seen, qw + g:qw + g + HEAD_SIZE]
            val = qkv_ref[0:seen, qw + kw + g:qw + kw + g + HEAD_SIZE]
            scores = lax.dot_general(q, key, (((1,), (1,)), ((), ())), preferred_element_type=jnp.float32)
            scores = jnp.where(causal, scores * HEAD_SIZE ** -0.5, -jnp.inf)
            weights = jnp.exp(scores - jnp.max(scores, axis=-1, keepdims=True))
            probs = (weights / jnp.sum(weights, axis=-1, keepdims=True)).astype(jnp.bfloat16)
            mixed = jnp.dot(probs, val, preferred_element_type=jnp.float32)
            out_ref[rows, h * HEAD_SIZE:(h + 1) * HEAD_SIZE] = jnp.where(live, mixed, 0.0).astype(jnp.bfloat16)


def body(n_t, n_r, tokens, lengths, block_adapter_index, cache_page_index, query_matrix, key_matrix, value_matrix,
         down_factors, query_up_factors, value_up_factors):
    T, F = tokens.shape[1:]
    qw, kw = query_matrix.shape[1], key_matrix.shape[1]
    per, rank = query_up_factors.shape[:2]
    bf16, f32 = jnp.bfloat16, jnp.float32
    aid = jnp.broadcast_to(block_adapter_index.reshape(1, 1), (T, 1))
    live = (jnp.arange(T, dtype=jnp.int32)[:, None] < lengths[0]).astype(jnp.int32)
    cosine, sine = rope_tables(T, HEAD_SIZE)
    n_x = n_r // 2
    vmem = pl.BlockSpec(memory_space=pltpu.VMEM)
    smem = pl.BlockSpec(memory_space=pltpu.SMEM)
    dma = pltpu.SemaphoreType.DMA
    qkv = pl.pallas_call(
        functools.partial(project_kernel, n_t, n_r),
        out_shape=jax.ShapeDtypeStruct((T, qw + 2 * kw), bf16),
        in_specs=[vmem] * 11,
        out_specs=vmem,
        scratch_shapes=[
            pltpu.VMEM((n_t, T, F), bf16),
            pltpu.VMEM((T, qw + 2 * kw), f32),
            pltpu.VMEM((n_r,) + down_factors.shape, bf16),
            pltpu.VMEM((n_r,) + query_up_factors.shape, bf16),
            pltpu.VMEM((n_r,) + value_up_factors.shape, bf16),
            pltpu.VMEM((T, 2 * rank), f32),
            pltpu.VMEM((n_t, T // n_t, 2 * rank), f32),
            pltpu.VMEM((T // n_t, 2 * rank), bf16),
            pltpu.VMEM((n_t, T // n_t, 2 * rank), bf16),
            dma((2, n_t - 1, CHUNKS)), dma((2, n_t - 1, CHUNKS)),
            dma((3, n_x, 2)), dma((3, n_x, 2)),
            dma((n_t,)), dma((n_t,)), dma((n_t,)), dma((n_t,)),
        ],
        compiler_params=pltpu.CompilerParams(
            collective_id=0, has_side_effects=True, vmem_limit_bytes=56 * 1024 * 1024),
        name="project",
    )(tokens[0], aid, live, jnp.asarray(cosine), jnp.asarray(sine), query_matrix, key_matrix, value_matrix,
      down_factors, query_up_factors, value_up_factors)
    attended, pages = pl.pallas_call(
        functools.partial(attend_kernel, qw, kw),
        out_shape=(
            jax.ShapeDtypeStruct((T, qw), bf16),
            jax.ShapeDtypeStruct((T // PAGE, 2, PAGE, kw), bf16),
        ),
        in_specs=[smem, smem, vmem],
        out_specs=(vmem, vmem),
        compiler_params=pltpu.CompilerParams(vmem_limit_bytes=48 * 1024 * 1024),
        name="attend",
    )(lengths, cache_page_index, qkv)
    return attended[None], pages[None]


def solution(mesh):
    in_specs = (
        P(("groups", "replica"), None, "tensor"),
        P(("groups", "replica")),
        P(("groups", "replica")),
        P(("groups", "replica"), None),
        P(None, "tensor"),
        P(None, "tensor"),
        P(None, "tensor"),
        P("replica", "tensor", None),
        P("replica", None, "tensor"),
        P("replica", None, "tensor"),
    )
    out_specs = (
        P(("groups", "replica"), None, "tensor"),
        P(("groups", "replica"), None, None, None, "tensor"),
    )
    return jax.shard_map(
        functools.partial(body, mesh.shape["tensor"], mesh.shape["replica"]),
        mesh=mesh, in_specs=in_specs, out_specs=out_specs, check_vma=False)
```

```python
import functools

import jax
import jax.numpy as jnp
import numpy as np
from jax import lax
from jax.experimental import pallas as pl
from jax.experimental.pallas import tpu as pltpu
from jax.sharding import PartitionSpec as P

HEAD_SIZE = 128
PAGE = 64
CHUNKS = 4


def rope_tables(length, width):
    half = width // 2
    exponent = np.float32(2.0) * np.arange(half, dtype=np.float32) / np.float32(width)
    frequency = np.exp(-np.log(np.float32(500000.0)) * exponent).astype(np.float32)
    angles = np.arange(length, dtype=np.float32)[:, None] * frequency[None, :]
    cosine, sine = np.cos(angles), np.sin(angles)
    terms = []
    for table in (np.concatenate([cosine, cosine], axis=1), np.concatenate([-sine, sine], axis=1)):
        rest = table.astype(np.float32)
        for _ in range(3):
            term = rest.astype(jnp.bfloat16)
            terms.append(term)
            rest = rest - term.astype(np.float32)
    return np.concatenate(terms, axis=1)


def project_kernel(
    n_t, n_r, x_ref, meta_ref, tab_ref, wq_ref, wk_ref, wv_ref, dn_ref, uq_ref, uv_ref,
    out_ref,
    meta, packed, mb, zb, xb, xg, acc, aid, rope, dg, ugq, ugv, part, pr, sh, shg, qg,
    ms, mr, as_, ar_, bs, br, zs, zr, asend, arecv, rs_s, rs_r, ag_s, ag_r, es, er,
):
    me = lax.axis_index("tensor")
    rep = lax.axis_index("replica")
    chip, core = rep // 2, rep % 2
    n_x = n_r // 2
    mate = chip * 2 + 1 - core
    B, F = x_ref.shape
    T = xg.shape[1]
    R = T // CHUNKS
    S = T // n_t
    per = dn_ref.shape[0]
    rank = uq_ref.shape[1]
    qw, kw = wq_ref.shape[1], wk_ref.shape[1]
    bf16, f32, i32 = jnp.bfloat16, jnp.float32, jnp.int32

    def tensor_peer(i):
        return lax.rem(me + i, n_t)

    def same_core(i):
        return lax.rem(chip + i, n_x) * 2 + core

    def from_chip(i):
        return lax.rem(chip + n_x - i, n_x)

    barrier = pltpu.get_barrier_semaphore()
    for i in range(1, n_t):
        pl.semaphore_signal(barrier, inc=1, device_id={"tensor": tensor_peer(i)})
    for i in range(1, n_r):
        pl.semaphore_signal(barrier, inc=1, device_id={"replica": lax.rem(rep + i, n_r)})
    pl.semaphore_wait(barrier, n_t - 1 + n_r - 1)

    def remote(src, dst, send, recv, **to):
        return pltpu.make_async_remote_copy(
            src_ref=src, dst_ref=dst, send_sem=send, recv_sem=recv, device_id=to)

    def rows_of(c):
        return pl.ds(pl.multiple_of(c * R, R), R)

    def meta_copy(i):
        return remote(meta_ref, meta.at[rep], ms.at[i], mr.at[i], replica=lax.rem(rep + i, n_r))

    for i in range(1, n_r):
        meta_copy(i).start()
    meta[rep] = meta_ref[...]
    for i in range(1, n_r):
        slot = lax.rem(rep + n_r - i, n_r)
        remote(meta.at[slot], meta.at[slot], ms.at[i], mr.at[i], replica=rep).wait_recv()
    own_len = meta_ref[0:1, :]
    offs = []
    total = jnp.zeros_like(own_len)
    own_off = total
    for r in range(n_r):
        offs.append(total)
        own_off = jnp.where(rep == r, total, own_off)
        total = total + meta[r, 0:1, :]

    def send_pack(c, carry):
        width = n_r * R
        g = lax.broadcasted_iota(i32, (width, B), 0)
        t = lax.broadcasted_iota(i32, (width, B), 1)
        owner = lax.rem(g // R, n_x) * 2 + g // (R * n_x)
        place = owner * T + c * R + lax.rem(g, R)
        pick = (place == t + own_off[:, 0:1]) & (t < own_len[:, 0:1])
        rows = jnp.dot(pick.astype(f32).astype(bf16), x_ref[...], preferred_element_type=f32)
        packed[c] = rows.astype(bf16).reshape(2, n_x, R, F)
        mate_copy(c).start()
        return carry

    def mate_copy(c):
        return remote(packed.at[c, 1 - core], mb.at[c], as_.at[c], ar_.at[c], replica=mate)

    def chip_copy(c, i):
        return remote(zb.at[c, lax.rem(chip + i, n_x)], xb.at[c, i], bs.at[c, i], br.at[c, i], replica=same_core(i))

    def send_chip(c, carry):
        mate_copy(c).wait_recv()
        zb[c] = packed[c, core] + mb[c]
        for i in range(1, n_x):
            chip_copy(c, i).start()
        return carry

    def pack_step(c, carry):
        send_pack(c, carry)
        send_chip(c - 1, carry)
        return carry

    send_pack(0, 0)
    lax.fori_loop(1, CHUNKS, pack_step, 0)
    send_chip(CHUNKS - 1, 0)

    pools = ((dn_ref, dg), (uq_ref, ugq), (uv_ref, ugv))

    def pool_copy(k, slot, i, j, to, own):
        src = pools[k][0] if own else pools[k][1].at[slot]
        return remote(src, pools[k][1].at[slot], asend.at[k, i, j], arecv.at[k, i, j], replica=to)

    for k in range(3):
        for i in range(1, n_x):
            pool_copy(k, rep, i, 0, same_core(i), True).start()
        pool_copy(k, rep, 0, 1, mate, True).start()
        pools[k][1][rep] = pools[k][0][...]

    def item(side, d, c):
        sgn = 1 - 2 * side
        ref = xg.at[me - sgn * d, rows_of(c)]
        return remote(ref, ref, zs.at[side, d, c], zr.at[side, d, c], tensor=me + sgn)

    def arrival(side, d, c):
        sgn = 1 - 2 * side
        ref = xg.at[me - sgn * d, rows_of(c)]
        return remote(ref, ref, zs.at[side, d - 1, c], zr.at[side, d - 1, c], tensor=me)

    def inside(t):
        return (t >= 0) & (t < n_t)

    def mac(src, c, first=False):
        rows = rows_of(c)
        x = xg[src, rows]
        feat = pl.ds(pl.multiple_of(src * F, F), F)
        lo = 0
        for w_ref in (wq_ref, wk_ref, wv_ref):
            width = w_ref.shape[1]
            term = jnp.dot(x, w_ref[feat, :], preferred_element_type=f32)
            if first:
                acc[rows, lo:lo + width] = term
            else:
                acc[rows, lo:lo + width] += term
            lo += width

    def send_own(c, carry):
        value = zb[c, chip]
        for i in range(1, n_x):
            chip_copy(c, i).wait_recv()
            value = value + xb[c, i]
        xg[me, rows_of(c)] = value
        for side in range(2):
            @pl.when(inside(me + 1 - 2 * side))
            def _():
                item(side, 0, c).start()
        mac(me, c, True)
        return carry

    lax.fori_loop(0, CHUNKS, send_own, 0)

    place = lax.broadcasted_iota(i32, (T, 128), 0) + rep * T
    ids = jnp.zeros((T, 128), i32)
    pos = jnp.zeros((T, 128), i32)
    for r in range(n_r):
        mine = (place >= offs[r]) & (place < offs[r] + meta[r, 0:1, :])
        ids = jnp.where(mine, meta[r, 1:2, :], ids)
        pos = jnp.where(mine, place - offs[r], pos)
    aid[...] = ids
    pick = lax.broadcasted_iota(i32, (T, B), 1) == pos[:, 0:1]
    found = jnp.dot(pick.astype(f32).astype(bf16), tab_ref[...], preferred_element_type=f32)
    H = HEAD_SIZE
    rope[0] = found[:, 0:H] + found[:, H:2 * H] + found[:, 2 * H:3 * H]
    rope[1] = found[:, 3 * H:4 * H] + found[:, 4 * H:5 * H] + found[:, 5 * H:6 * H]

    def return_copy(slot, c, i, j, to):
        ref = qg.at[slot, rows_of(c)]
        return remote(ref, ref, es.at[c, i, j], er.at[c, i, j], replica=to)

    def finish(c):
        rows = rows_of(c)
        for lo in range(0, qw + 2 * kw, H):
            v = acc[rows, lo:lo + H]
            if lo < qw + kw:
                v = v * rope[0, rows] + pltpu.roll(v, H // 2, 1) * rope[1, rows]
            qg[rep, rows, lo:lo + H] = v.astype(bf16)
        for i in range(1, n_x):
            return_copy(rep, c, i, 0, same_core(i)).start()
        return_copy(rep, c, 0, 1, mate).start()

    def pass_on(c):
        for i in range(1, n_x):
            slot = from_chip(i) * 2 + core
            return_copy(slot, c, i, 0, rep).wait_recv()
            return_copy(slot, c, i, 1, mate).start()

    def phase(first, last, end=False):
        def step(k, carry):
            d, c = k // CHUNKS + 1, lax.rem(k, CHUNKS)

            def one(side, carry):
                sgn = 1 - 2 * side
                src = me - sgn * d

                @pl.when(inside(src))
                def _():
                    arrival(side, d, c).wait_recv()
                    if not end:
                        @pl.when(inside(me + sgn))
                        def _():
                            item(side, d, c).start()

                    mac(src, c)

                return carry

            lax.fori_loop(0, 2, one, 0)
            if end:
                finish(c)

                @pl.when(c > 0)
                def _():
                    pass_on(c - 1)

            return carry

        lax.fori_loop(first, last, step, 0)

    cut = min(CHUNKS + CHUNKS // 2, (n_t - 2) * CHUNKS)
    phase(0, cut)

    for i in range(1, n_x):
        slot = from_chip(i) * 2 + core
        for k in range(3):
            pool_copy(k, slot, i, 0, mate, False).wait_recv()
            pool_copy(k, slot, i, 1, mate, False).start()
    for i in range(n_x):
        slot = from_chip(i) * 2 + 1 - core
        for k in range(3):
            pool_copy(k, slot, i, 1, mate, False).wait_recv()

    part[...] = jnp.zeros_like(part)

    def down(a, carry):
        term = jnp.dot(xg[me], dg[a // per, lax.rem(a, per)], preferred_element_type=f32)
        part[...] += jnp.where(aid[...] == a, term, 0.0)
        return carry

    lax.fori_loop(0, n_r * per, down, 0)

    def share(t):
        return pl.ds(pl.multiple_of(t * S, S), S)

    def rs_copy(i):
        t = tensor_peer(i)
        return remote(part.at[share(t)], pr.at[me], rs_s.at[i], rs_r.at[i], tensor=t)

    def ag_copy(i):
        return remote(sh, shg.at[share(me)], ag_s.at[i], ag_r.at[i], tensor=tensor_peer(i))

    for i in range(1, n_t):
        rs_copy(i).start()
    pr[me] = part[share(me)]

    phase(cut, (n_t - 2) * CHUNKS)

    for i in range(1, n_t):
        ref = pr.at[lax.rem(me + n_t - i, n_t)]
        remote(ref, ref, rs_s.at[i], rs_r.at[i], tensor=me).wait_recv()
    summed = pr[0]
    for t in range(1, n_t):
        summed = summed + pr[t]
    sh[...] = summed.astype(bf16)
    for i in range(1, n_t):
        ag_copy(i).start()
    shg[share(me)] = sh[...]
    for i in range(1, n_t):
        ref = shg.at[share(lax.rem(me + n_t - i, n_t))]
        remote(ref, ref, ag_s.at[i], ag_r.at[i], tensor=me).wait_recv()

    def up(a, carry):
        mine = jnp.where(aid[...] == a, shg[...].astype(f32), 0.0).astype(bf16)
        acc[:, 0:qw] += jnp.dot(mine[:, :rank], ugq[a // per, lax.rem(a, per)], preferred_element_type=f32)
        acc[:, qw + kw:] += jnp.dot(mine[:, rank:], ugv[a // per, lax.rem(a, per)], preferred_element_type=f32)
        return carry

    lax.fori_loop(0, n_r * per, up, 0)

    phase((n_t - 2) * CHUNKS, (n_t - 1) * CHUNKS, True)
    pass_on(CHUNKS - 1)

    for c in range(CHUNKS):
        for i in range(n_x):
            return_copy(from_chip(i) * 2 + 1 - core, c, i, 1, rep).wait_recv()

    tile = 256

    def unpack(k, carry):
        t = lax.broadcasted_iota(i32, (tile, T), 0) + k * tile
        g = lax.broadcasted_iota(i32, (tile, T), 1)
        rows = None
        for r in range(n_r):
            pick = (g + r * T == t + own_off[:, 0:1]) & (t < own_len[:, 0:1])
            term = jnp.dot(pick.astype(f32).astype(bf16), qg[r], preferred_element_type=f32)
            rows = term if rows is None else rows + term
        out_ref[pl.ds(pl.multiple_of(k * tile, tile), tile), :] = rows.astype(bf16)
        return carry

    lax.fori_loop(0, B // tile, unpack, 0)

    def drain(k, carry):
        d, c = k // CHUNKS, lax.rem(k, CHUNKS)
        for side in range(2):
            sgn = 1 - 2 * side

            @pl.when(inside(me - sgn * d) & inside(me + sgn))
            def _():
                item(side, d, c).wait_send()
        return carry

    lax.fori_loop(0, (n_t - 1) * CHUNKS, drain, 0)
    for i in range(1, n_t):
        rs_copy(i).wait_send()
        ag_copy(i).wait_send()
    for i in range(1, n_r):
        meta_copy(i).wait_send()
    for k in range(3):
        pool_copy(k, rep, 0, 1, mate, True).wait_send()
        for i in range(1, n_x):
            pool_copy(k, rep, i, 0, same_core(i), True).wait_send()
            pool_copy(k, from_chip(i) * 2 + core, i, 1, mate, False).wait_send()

    def drain_chunk(c, carry):
        mate_copy(c).wait_send()
        return_copy(rep, c, 0, 1, mate).wait_send()
        for i in range(1, n_x):
            chip_copy(c, i).wait_send()
            return_copy(rep, c, i, 0, same_core(i)).wait_send()
            return_copy(from_chip(i) * 2 + core, c, i, 1, mate).wait_send()
        return carry

    lax.fori_loop(0, CHUNKS, drain_chunk, 0)


def attend_kernel(qw, kw, length_ref, page_ref, qkv_ref, out_ref, pages_ref):
    T = qkv_ref.shape[0]
    tile = 256
    group = qw // kw
    length = length_ref[0]
    for p in range(T // PAGE):
        at = page_ref[0, p]
        pages_ref[at, 0] = qkv_ref[p * PAGE:(p + 1) * PAGE, qw:qw + kw]
        pages_ref[at, 1] = qkv_ref[p * PAGE:(p + 1) * PAGE, qw + kw:]
    for i in range(T // tile):
        rows = slice(i * tile, (i + 1) * tile)
        seen = (i + 1) * tile
        t = lax.broadcasted_iota(jnp.int32, (tile, seen), 0) + i * tile
        s = lax.broadcasted_iota(jnp.int32, (tile, seen), 1)
        causal = s <= t
        live = lax.broadcasted_iota(jnp.int32, (tile, HEAD_SIZE), 0) + i * tile < length
        for h in range(qw // HEAD_SIZE):
            g = (h // group) * HEAD_SIZE
            q = qkv_ref[rows, h * HEAD_SIZE:(h + 1) * HEAD_SIZE]
            key = qkv_ref[0:seen, qw + g:qw + g + HEAD_SIZE]
            val = qkv_ref[0:seen, qw + kw + g:qw + kw + g + HEAD_SIZE]
            scores = lax.dot_general(q, key, (((1,), (1,)), ((), ())), preferred_element_type=jnp.float32)
            scores = jnp.where(causal, scores * HEAD_SIZE ** -0.5, -jnp.inf)
            weights = jnp.exp(scores - jnp.max(scores, axis=-1, keepdims=True))
            probs = (weights / jnp.sum(weights, axis=-1, keepdims=True)).astype(jnp.bfloat16)
            mixed = jnp.dot(probs, val, preferred_element_type=jnp.float32)
            out_ref[rows, h * HEAD_SIZE:(h + 1) * HEAD_SIZE] = jnp.where(live, mixed, 0.0).astype(jnp.bfloat16)


def body(n_t, n_r, tokens, lengths, block_adapter_index, cache_page_index, query_matrix, key_matrix, value_matrix,
         down_factors, query_up_factors, value_up_factors):
    B, F = tokens.shape[1:]
    T = B // 2
    R = T // CHUNKS
    qw, kw = query_matrix.shape[1], key_matrix.shape[1]
    W = qw + 2 * kw
    rank = query_up_factors.shape[1]
    bf16, f32, i32 = jnp.bfloat16, jnp.float32, jnp.int32
    pair = jnp.concatenate([lengths, block_adapter_index, jnp.zeros((6,), i32)])
    meta = jnp.broadcast_to(pair[:, None], (8, 128))
    n_x = n_r // 2
    vmem = pl.BlockSpec(memory_space=pltpu.VMEM)
    smem = pl.BlockSpec(memory_space=pltpu.SMEM)
    dma = pltpu.SemaphoreType.DMA
    qkv = pl.pallas_call(
        functools.partial(project_kernel, n_t, n_r),
        out_shape=jax.ShapeDtypeStruct((B, W), bf16),
        in_specs=[vmem] * 9,
        out_specs=vmem,
        scratch_shapes=[
            pltpu.VMEM((n_r, 8, 128), i32),
            pltpu.VMEM((CHUNKS, 2, n_x, R, F), bf16),
            pltpu.VMEM((CHUNKS, n_x, R, F), bf16),
            pltpu.VMEM((CHUNKS, n_x, R, F), bf16),
            pltpu.VMEM((CHUNKS, n_x, R, F), bf16),
            pltpu.VMEM((n_t, T, F), bf16),
            pltpu.VMEM((T, W), f32),
            pltpu.VMEM((T, 128), i32),
            pltpu.VMEM((2, T, HEAD_SIZE), f32),
            pltpu.VMEM((n_r,) + down_factors.shape, bf16),
            pltpu.VMEM((n_r,) + query_up_factors.shape, bf16),
            pltpu.VMEM((n_r,) + value_up_factors.shape, bf16),
            pltpu.VMEM((T, 2 * rank), f32),
            pltpu.VMEM((n_t, T // n_t, 2 * rank), f32),
            pltpu.VMEM((T // n_t, 2 * rank), bf16),
            pltpu.VMEM((T, 2 * rank), bf16),
            pltpu.VMEM((n_r, T, W), bf16),
            dma((n_r,)), dma((n_r,)),
            dma((CHUNKS,)), dma((CHUNKS,)),
            dma((CHUNKS, n_x)), dma((CHUNKS, n_x)),
            dma((2, n_t - 1, CHUNKS)), dma((2, n_t - 1, CHUNKS)),
            dma((3, n_x, 2)), dma((3, n_x, 2)),
            dma((n_t,)), dma((n_t,)), dma((n_t,)), dma((n_t,)),
            dma((CHUNKS, n_x, 2)), dma((CHUNKS, n_x, 2)),
        ],
        compiler_params=pltpu.CompilerParams(
            collective_id=0, has_side_effects=True, vmem_limit_bytes=58 * 1024 * 1024),
        name="project",
    )(tokens[0], meta, jnp.asarray(rope_tables(B, HEAD_SIZE)), query_matrix, key_matrix, value_matrix,
      down_factors, query_up_factors, value_up_factors)
    attended, pages = pl.pallas_call(
        functools.partial(attend_kernel, qw, kw),
        out_shape=(
            jax.ShapeDtypeStruct((B, qw), bf16),
            jax.ShapeDtypeStruct((B // PAGE, 2, PAGE, kw), bf16),
        ),
        in_specs=[smem, smem, vmem],
        out_specs=(vmem, vmem),
        compiler_params=pltpu.CompilerParams(vmem_limit_bytes=48 * 1024 * 1024),
        name="attend",
    )(lengths, cache_page_index, qkv)
    return attended[None], pages[None]


def solution(mesh):
    in_specs = (
        P(("groups", "replica"), None, "tensor"),
        P(("groups", "replica")),
        P(("groups", "replica")),
        P(("groups", "replica"), None),
        P(None, "tensor"),
        P(None, "tensor"),
        P(None, "tensor"),
        P("replica", "tensor", None),
        P("replica", None, "tensor"),
        P("replica", None, "tensor"),
    )
    out_specs = (
        P(("groups", "replica"), None, "tensor"),
        P(("groups", "replica"), None, None, None, "tensor"),
    )
    return jax.shard_map(
        functools.partial(body, mesh.shape["tensor"], mesh.shape["replica"]),
        mesh=mesh, in_specs=in_specs, out_specs=out_specs, check_vma=False)
```

```python
import functools

import jax
import jax.numpy as jnp
import numpy as np
from jax import lax
from jax.experimental import pallas as pl
from jax.experimental.pallas import tpu as pltpu
from jax.sharding import PartitionSpec as P

HEAD_SIZE = 128
PAGE = 64
CHUNKS = 4


def rope_tables(length, width):
    half = width // 2
    exponent = np.float32(2.0) * np.arange(half, dtype=np.float32) / np.float32(width)
    frequency = np.exp(-np.log(np.float32(500000.0)) * exponent).astype(np.float32)
    angles = np.arange(length, dtype=np.float32)[:, None] * frequency[None, :]
    cosine, sine = np.cos(angles), np.sin(angles)
    terms = []
    for table in (np.concatenate([cosine, cosine], axis=1), np.concatenate([-sine, sine], axis=1)):
        rest = table.astype(np.float32)
        for _ in range(3):
            term = rest.astype(jnp.bfloat16)
            terms.append(term)
            rest = rest - term.astype(np.float32)
    return np.concatenate(terms, axis=1)


def project_kernel(
    n_t, n_r, x_ref, meta_ref, tab_hbm, wq_hbm, wk_hbm, wv_hbm, dn_ref, uq_ref, uv_ref,
    out_ref,
    meta, packed, mb, zb, xb, xg, acc, aid, rope, dg, ugq, ugv, part, pr, sh, shg, qg,
    ms, mr, as_, ar_, bs, br, zs, zr, asend, arecv, rs_s, rs_r, ag_s, ag_r, es, er,
    tab_ref, wq_ref, wk_ref, wv_ref, ws,
):
    me = lax.axis_index("tensor")
    rep = lax.axis_index("replica")
    chip, core = rep // 2, rep % 2
    n_x = n_r // 2
    mate = chip * 2 + 1 - core
    B, F = x_ref.shape
    T = xg.shape[1]
    R = T // CHUNKS
    S = T // n_t
    per = dn_ref.shape[0]
    rank = uq_ref.shape[1]
    qw, kw = wq_ref.shape[1], wk_ref.shape[1]
    bf16, f32, i32 = jnp.bfloat16, jnp.float32, jnp.int32

    def tensor_peer(i):
        return lax.rem(me + i, n_t)

    def same_core(i):
        return lax.rem(chip + i, n_x) * 2 + core

    def from_chip(i):
        return lax.rem(chip + n_x - i, n_x)

    loads = [
        pltpu.make_async_copy(src, dst, ws.at[k])
        for k, (src, dst) in enumerate(
            ((wq_hbm, wq_ref), (wk_hbm, wk_ref), (wv_hbm, wv_ref), (tab_hbm, tab_ref)))
    ]
    for load in loads:
        load.start()

    barrier = pltpu.get_barrier_semaphore()
    for i in range(1, n_t):
        pl.semaphore_signal(barrier, inc=1, device_id={"tensor": tensor_peer(i)})
    for i in range(1, n_r):
        pl.semaphore_signal(barrier, inc=1, device_id={"replica": lax.rem(rep + i, n_r)})
    pl.semaphore_wait(barrier, n_t - 1 + n_r - 1)

    def remote(src, dst, send, recv, **to):
        return pltpu.make_async_remote_copy(
            src_ref=src, dst_ref=dst, send_sem=send, recv_sem=recv, device_id=to)

    def rows_of(c):
        return pl.ds(pl.multiple_of(c * R, R), R)

    def meta_copy(i):
        return remote(meta_ref, meta.at[rep], ms.at[i], mr.at[i], replica=lax.rem(rep + i, n_r))

    for i in range(1, n_r):
        meta_copy(i).start()
    meta[rep] = meta_ref[...]
    for i in range(1, n_r):
        slot = lax.rem(rep + n_r - i, n_r)
        remote(meta.at[slot], meta.at[slot], ms.at[i], mr.at[i], replica=rep).wait_recv()
    own_len = meta_ref[0:1, :]
    offs = []
    total = jnp.zeros_like(own_len)
    own_off = total
    for r in range(n_r):
        offs.append(total)
        own_off = jnp.where(rep == r, total, own_off)
        total = total + meta[r, 0:1, :]

    def send_pack(c, carry):
        width = n_r * R
        g = lax.broadcasted_iota(i32, (width, B), 0)
        t = lax.broadcasted_iota(i32, (width, B), 1)
        owner = lax.rem(g // R, n_x) * 2 + g // (R * n_x)
        place = owner * T + c * R + lax.rem(g, R)
        pick = (place == t + own_off[:, 0:1]) & (t < own_len[:, 0:1])
        rows = jnp.dot(pick.astype(f32).astype(bf16), x_ref[...], preferred_element_type=f32)
        packed[c] = rows.astype(bf16).reshape(2, n_x, R, F)
        mate_copy(c).start()
        return carry

    def mate_copy(c):
        return remote(packed.at[c, 1 - core], mb.at[c], as_.at[c], ar_.at[c], replica=mate)

    def chip_copy(c, i):
        return remote(zb.at[c, lax.rem(chip + i, n_x)], xb.at[c, i], bs.at[c, i], br.at[c, i], replica=same_core(i))

    def send_chip(c, carry):
        mate_copy(c).wait_recv()
        zb[c] = packed[c, core] + mb[c]
        for i in range(1, n_x):
            chip_copy(c, i).start()
        return carry

    def pack_step(c, carry):
        send_pack(c, carry)
        send_chip(c - 1, carry)
        return carry

    send_pack(0, 0)
    lax.fori_loop(1, CHUNKS, pack_step, 0)
    send_chip(CHUNKS - 1, 0)

    pools = ((dn_ref, dg), (uq_ref, ugq), (uv_ref, ugv))

    def pool_copy(k, slot, i, j, to, own):
        src = pools[k][0] if own else pools[k][1].at[slot]
        return remote(src, pools[k][1].at[slot], asend.at[k, i, j], arecv.at[k, i, j], replica=to)

    for k in range(3):
        for i in range(1, n_x):
            pool_copy(k, rep, i, 0, same_core(i), True).start()
        pool_copy(k, rep, 0, 1, mate, True).start()
        pools[k][1][rep] = pools[k][0][...]

    def item(side, d, c):
        sgn = 1 - 2 * side
        ref = xg.at[me - sgn * d, rows_of(c)]
        return remote(ref, ref, zs.at[side, d, c], zr.at[side, d, c], tensor=me + sgn)

    def arrival(side, d, c):
        sgn = 1 - 2 * side
        ref = xg.at[me - sgn * d, rows_of(c)]
        return remote(ref, ref, zs.at[side, d - 1, c], zr.at[side, d - 1, c], tensor=me)

    def inside(t):
        return (t >= 0) & (t < n_t)

    def mac(src, c, first=False):
        rows = rows_of(c)
        x = xg[src, rows]
        feat = pl.ds(pl.multiple_of(src * F, F), F)
        lo = 0
        for w_ref in (wq_ref, wk_ref, wv_ref):
            width = w_ref.shape[1]
            term = jnp.dot(x, w_ref[feat, :], preferred_element_type=f32)
            if first:
                acc[rows, lo:lo + width] = term
            else:
                acc[rows, lo:lo + width] += term
            lo += width

    def send_own(c, carry):
        value = zb[c, chip]
        for i in range(1, n_x):
            chip_copy(c, i).wait_recv()
            value = value + xb[c, i]
        xg[me, rows_of(c)] = value
        for side in range(2):
            @pl.when(inside(me + 1 - 2 * side))
            def _():
                item(side, 0, c).start()
        mac(me, c, True)
        return carry

    for load in loads:
        load.wait()
    lax.fori_loop(0, CHUNKS, send_own, 0)

    place = lax.broadcasted_iota(i32, (T, 128), 0) + rep * T
    ids = jnp.zeros((T, 128), i32)
    pos = jnp.zeros((T, 128), i32)
    for r in range(n_r):
        mine = (place >= offs[r]) & (place < offs[r] + meta[r, 0:1, :])
        ids = jnp.where(mine, meta[r, 1:2, :], ids)
        pos = jnp.where(mine, place - offs[r], pos)
    aid[...] = ids
    pick = lax.broadcasted_iota(i32, (T, B), 1) == pos[:, 0:1]
    found = jnp.dot(pick.astype(f32).astype(bf16), tab_ref[...], preferred_element_type=f32)
    H = HEAD_SIZE
    rope[0] = found[:, 0:H] + found[:, H:2 * H] + found[:, 2 * H:3 * H]
    rope[1] = found[:, 3 * H:4 * H] + found[:, 4 * H:5 * H] + found[:, 5 * H:6 * H]

    def return_copy(slot, c, i, j, to):
        ref = qg.at[slot, rows_of(c)]
        return remote(ref, ref, es.at[c, i, j], er.at[c, i, j], replica=to)

    def finish(c):
        rows = rows_of(c)
        for lo in range(0, qw + 2 * kw, H):
            v = acc[rows, lo:lo + H]
            if lo < qw + kw:
                v = v * rope[0, rows] + pltpu.roll(v, H // 2, 1) * rope[1, rows]
            qg[rep, rows, lo:lo + H] = v.astype(bf16)
        for i in range(1, n_x):
            return_copy(rep, c, i, 0, same_core(i)).start()
        return_copy(rep, c, 0, 1, mate).start()

    def pass_on(c):
        for i in range(1, n_x):
            slot = from_chip(i) * 2 + core
            return_copy(slot, c, i, 0, rep).wait_recv()
            return_copy(slot, c, i, 1, mate).start()

    def phase(first, last, end=False):
        def step(k, carry):
            d, c = k // CHUNKS + 1, lax.rem(k, CHUNKS)

            def one(side, carry):
                sgn = 1 - 2 * side
                src = me - sgn * d

                @pl.when(inside(src))
                def _():
                    arrival(side, d, c).wait_recv()
                    if not end:
                        @pl.when(inside(me + sgn))
                        def _():
                            item(side, d, c).start()

                    mac(src, c)

                return carry

            lax.fori_loop(0, 2, one, 0)
            if end:
                finish(c)

                @pl.when(c > 0)
                def _():
                    pass_on(c - 1)

            return carry

        lax.fori_loop(first, last, step, 0)

    phase(0, (n_t - 2) * CHUNKS)

    for i in range(1, n_x):
        slot = from_chip(i) * 2 + core
        for k in range(3):
            pool_copy(k, slot, i, 0, mate, False).wait_recv()
            pool_copy(k, slot, i, 1, mate, False).start()
    for i in range(n_x):
        slot = from_chip(i) * 2 + 1 - core
        for k in range(3):
            pool_copy(k, slot, i, 1, mate, False).wait_recv()

    part[...] = jnp.zeros_like(part)

    def down(a, carry):
        term = jnp.dot(xg[me], dg[a // per, lax.rem(a, per)], preferred_element_type=f32)
        part[...] += jnp.where(aid[...] == a, term, 0.0)
        return carry

    lax.fori_loop(0, n_r * per, down, 0)

    def share(t):
        return pl.ds(pl.multiple_of(t * S, S), S)

    def rs_copy(i):
        t = tensor_peer(i)
        return remote(part.at[share(t)], pr.at[me], rs_s.at[i], rs_r.at[i], tensor=t)

    def ag_copy(i):
        return remote(sh, shg.at[share(me)], ag_s.at[i], ag_r.at[i], tensor=tensor_peer(i))

    for i in range(1, n_t):
        rs_copy(i).start()
    pr[me] = part[share(me)]

    for i in range(1, n_t):
        ref = pr.at[lax.rem(me + n_t - i, n_t)]
        remote(ref, ref, rs_s.at[i], rs_r.at[i], tensor=me).wait_recv()
    summed = pr[0]
    for t in range(1, n_t):
        summed = summed + pr[t]
    sh[...] = summed.astype(bf16)
    for i in range(1, n_t):
        ag_copy(i).start()
    shg[share(me)] = sh[...]
    for i in range(1, n_t):
        ref = shg.at[share(lax.rem(me + n_t - i, n_t))]
        remote(ref, ref, ag_s.at[i], ag_r.at[i], tensor=me).wait_recv()

    def up(a, carry):
        mine = jnp.where(aid[...] == a, shg[...].astype(f32), 0.0).astype(bf16)
        acc[:, 0:qw] += jnp.dot(mine[:, :rank], ugq[a // per, lax.rem(a, per)], preferred_element_type=f32)
        acc[:, qw + kw:] += jnp.dot(mine[:, rank:], ugv[a // per, lax.rem(a, per)], preferred_element_type=f32)
        return carry

    lax.fori_loop(0, n_r * per, up, 0)

    phase((n_t - 2) * CHUNKS, (n_t - 1) * CHUNKS, True)
    pass_on(CHUNKS - 1)

    for c in range(CHUNKS):
        for i in range(n_x):
            return_copy(from_chip(i) * 2 + 1 - core, c, i, 1, rep).wait_recv()

    tile = 256

    def unpack(k, carry):
        t = lax.broadcasted_iota(i32, (tile, T), 0) + k * tile
        g = lax.broadcasted_iota(i32, (tile, T), 1)
        rows = None
        for r in range(n_r):
            pick = (g + r * T == t + own_off[:, 0:1]) & (t < own_len[:, 0:1])
            term = jnp.dot(pick.astype(f32).astype(bf16), qg[r], preferred_element_type=f32)
            rows = term if rows is None else rows + term
        out_ref[pl.ds(pl.multiple_of(k * tile, tile), tile), :] = rows.astype(bf16)
        return carry

    lax.fori_loop(0, B // tile, unpack, 0)

    def drain(k, carry):
        d, c = k // CHUNKS, lax.rem(k, CHUNKS)
        for side in range(2):
            sgn = 1 - 2 * side

            @pl.when(inside(me - sgn * d) & inside(me + sgn))
            def _():
                item(side, d, c).wait_send()
        return carry

    lax.fori_loop(0, (n_t - 1) * CHUNKS, drain, 0)
    for i in range(1, n_t):
        rs_copy(i).wait_send()
        ag_copy(i).wait_send()
    for i in range(1, n_r):
        meta_copy(i).wait_send()
    for k in range(3):
        pool_copy(k, rep, 0, 1, mate, True).wait_send()
        for i in range(1, n_x):
            pool_copy(k, rep, i, 0, same_core(i), True).wait_send()
            pool_copy(k, from_chip(i) * 2 + core, i, 1, mate, False).wait_send()

    def drain_chunk(c, carry):
        mate_copy(c).wait_send()
        return_copy(rep, c, 0, 1, mate).wait_send()
        for i in range(1, n_x):
            chip_copy(c, i).wait_send()
            return_copy(rep, c, i, 0, same_core(i)).wait_send()
            return_copy(from_chip(i) * 2 + core, c, i, 1, mate).wait_send()
        return carry

    lax.fori_loop(0, CHUNKS, drain_chunk, 0)


def attend_kernel(qw, kw, length_ref, page_ref, qkv_ref, out_ref, pages_ref):
    T = qkv_ref.shape[0]
    tile = 256
    group = qw // kw
    length = length_ref[0]
    for p in range(T // PAGE):
        at = page_ref[0, p]
        pages_ref[at, 0] = qkv_ref[p * PAGE:(p + 1) * PAGE, qw:qw + kw]
        pages_ref[at, 1] = qkv_ref[p * PAGE:(p + 1) * PAGE, qw + kw:]
    for i in range(T // tile):
        rows = slice(i * tile, (i + 1) * tile)
        past = i * tile
        t = lax.broadcasted_iota(jnp.int32, (tile, tile), 0)
        causal = lax.broadcasted_iota(jnp.int32, (tile, tile), 1) <= t
        live = lax.broadcasted_iota(jnp.int32, (tile, HEAD_SIZE), 0) + i * tile < length
        for h in range(qw // HEAD_SIZE):
            g = (h // group) * HEAD_SIZE
            q = qkv_ref[rows, h * HEAD_SIZE:(h + 1) * HEAD_SIZE]
            pieces = [(past, past + tile, True)] + ([(0, past, False)] if past else [])
            scores = []
            for lo, hi, diagonal in pieces:
                key = qkv_ref[lo:hi, qw + g:qw + g + HEAD_SIZE]
                piece = lax.dot_general(q, key, (((1,), (1,)), ((), ())), preferred_element_type=jnp.float32)
                scores.append(jnp.where(causal, piece, -jnp.inf) if diagonal else piece)
            peak = functools.reduce(jnp.maximum, [jnp.max(p, axis=-1, keepdims=True) for p in scores])
            weights = [jnp.exp((p - peak) * HEAD_SIZE ** -0.5) for p in scores]
            inverse = 1.0 / sum(jnp.sum(w, axis=-1, keepdims=True) for w in weights)
            mixed = jnp.zeros((tile, HEAD_SIZE), jnp.float32)
            for (lo, hi, _), w in zip(pieces, weights):
                val = qkv_ref[lo:hi, qw + kw + g:qw + kw + g + HEAD_SIZE]
                mixed = mixed + jnp.dot((w * inverse).astype(jnp.bfloat16), val, preferred_element_type=jnp.float32)
            out_ref[rows, h * HEAD_SIZE:(h + 1) * HEAD_SIZE] = jnp.where(live, mixed, 0.0).astype(jnp.bfloat16)


def body(n_t, n_r, tokens, lengths, block_adapter_index, cache_page_index, query_matrix, key_matrix, value_matrix,
         down_factors, query_up_factors, value_up_factors):
    B, F = tokens.shape[1:]
    T = B // 2
    R = T // CHUNKS
    qw, kw = query_matrix.shape[1], key_matrix.shape[1]
    W = qw + 2 * kw
    rank = query_up_factors.shape[1]
    bf16, f32, i32 = jnp.bfloat16, jnp.float32, jnp.int32
    pair = jnp.concatenate([lengths, block_adapter_index, jnp.zeros((6,), i32)])
    meta = jnp.broadcast_to(pair[:, None], (8, 128))
    n_x = n_r // 2
    vmem = pl.BlockSpec(memory_space=pltpu.VMEM)
    smem = pl.BlockSpec(memory_space=pltpu.SMEM)
    dma = pltpu.SemaphoreType.DMA
    qkv = pl.pallas_call(
        functools.partial(project_kernel, n_t, n_r),
        out_shape=jax.ShapeDtypeStruct((B, W), bf16),
        in_specs=[vmem] * 2 + [pl.BlockSpec(memory_space=pl.ANY)] * 4 + [vmem] * 3,
        out_specs=vmem,
        scratch_shapes=[
            pltpu.VMEM((n_r, 8, 128), i32),
            pltpu.VMEM((CHUNKS, 2, n_x, R, F), bf16),
            pltpu.VMEM((CHUNKS, n_x, R, F), bf16),
            pltpu.VMEM((CHUNKS, n_x, R, F), bf16),
            pltpu.VMEM((CHUNKS, n_x, R, F), bf16),
            pltpu.VMEM((n_t, T, F), bf16),
            pltpu.VMEM((T, W), f32),
            pltpu.VMEM((T, 128), i32),
            pltpu.VMEM((2, T, HEAD_SIZE), f32),
            pltpu.VMEM((n_r,) + down_factors.shape, bf16),
            pltpu.VMEM((n_r,) + query_up_factors.shape, bf16),
            pltpu.VMEM((n_r,) + value_up_factors.shape, bf16),
            pltpu.VMEM((T, 2 * rank), f32),
            pltpu.VMEM((n_t, T // n_t, 2 * rank), f32),
            pltpu.VMEM((T // n_t, 2 * rank), bf16),
            pltpu.VMEM((T, 2 * rank), bf16),
            pltpu.VMEM((n_r, T, W), bf16),
            dma((n_r,)), dma((n_r,)),
            dma((CHUNKS,)), dma((CHUNKS,)),
            dma((CHUNKS, n_x)), dma((CHUNKS, n_x)),
            dma((2, n_t - 1, CHUNKS)), dma((2, n_t - 1, CHUNKS)),
            dma((3, n_x, 2)), dma((3, n_x, 2)),
            dma((n_t,)), dma((n_t,)), dma((n_t,)), dma((n_t,)),
            dma((CHUNKS, n_x, 2)), dma((CHUNKS, n_x, 2)),
            pltpu.VMEM((B, 6 * HEAD_SIZE), bf16),
            pltpu.VMEM(query_matrix.shape, bf16),
            pltpu.VMEM(key_matrix.shape, bf16),
            pltpu.VMEM(value_matrix.shape, bf16),
            dma((4,)),
        ],
        compiler_params=pltpu.CompilerParams(
            collective_id=0, has_side_effects=True, vmem_limit_bytes=58 * 1024 * 1024),
        name="project",
    )(tokens[0], meta, jnp.asarray(rope_tables(B, HEAD_SIZE)), query_matrix, key_matrix, value_matrix,
      down_factors, query_up_factors, value_up_factors)
    attended, pages = pl.pallas_call(
        functools.partial(attend_kernel, qw, kw),
        out_shape=(
            jax.ShapeDtypeStruct((B, qw), bf16),
            jax.ShapeDtypeStruct((B // PAGE, 2, PAGE, kw), bf16),
        ),
        in_specs=[smem, smem, vmem],
        out_specs=(vmem, vmem),
        compiler_params=pltpu.CompilerParams(vmem_limit_bytes=48 * 1024 * 1024),
        name="attend",
    )(lengths, cache_page_index, qkv)
    return attended[None], pages[None]


def solution(mesh):
    in_specs = (
        P(("groups", "replica"), None, "tensor"),
        P(("groups", "replica")),
        P(("groups", "replica")),
        P(("groups", "replica"), None),
        P(None, "tensor"),
        P(None, "tensor"),
        P(None, "tensor"),
        P("replica", "tensor", None),
        P("replica", None, "tensor"),
        P("replica", None, "tensor"),
    )
    out_specs = (
        P(("groups", "replica"), None, "tensor"),
        P(("groups", "replica"), None, None, None, "tensor"),
    )
    return jax.shard_map(
        functools.partial(body, mesh.shape["tensor"], mesh.shape["replica"]),
        mesh=mesh, in_specs=in_specs, out_specs=out_specs, check_vma=False)
```

```python
import functools

import jax
import jax.numpy as jnp
import numpy as np
from jax import lax
from jax.experimental import pallas as pl
from jax.experimental.pallas import tpu as pltpu
from jax.sharding import PartitionSpec as P

HEAD_SIZE = 128
PAGE = 64
CHUNKS = 6


def rope_tables(length, width):
    half = width // 2
    exponent = np.float32(2.0) * np.arange(half, dtype=np.float32) / np.float32(width)
    frequency = np.exp(-np.log(np.float32(500000.0)) * exponent).astype(np.float32)
    angles = np.arange(length, dtype=np.float32)[:, None] * frequency[None, :]
    cosine, sine = np.cos(angles), np.sin(angles)
    terms = []
    for table in (np.concatenate([cosine, cosine], axis=1), np.concatenate([-sine, sine], axis=1)):
        rest = table.astype(np.float32)
        for _ in range(3):
            term = rest.astype(jnp.bfloat16)
            terms.append(term)
            rest = rest - term.astype(np.float32)
    return np.concatenate(terms, axis=1)


def project_kernel(
    n_t, n_r, x_ref, meta_ref, tab_hbm, wq_hbm, wk_hbm, wv_hbm, dn_ref, uq_ref, uv_ref,
    out_ref,
    meta, packed, mb, zb, xb, xg, acc, aid, rope, dg, ugq, ugv, part, pr, sh, shg, qg,
    ms, mr, as_, ar_, bs, br, zs, zr, asend, arecv, rs_s, rs_r, ag_s, ag_r, es, er,
    tab_ref, wq_ref, wk_ref, wv_ref, ws,
):
    me = lax.axis_index("tensor")
    rep = lax.axis_index("replica")
    chip, core = rep // 2, rep % 2
    n_x = n_r // 2
    mate = chip * 2 + 1 - core
    B, F = x_ref.shape
    T = xg.shape[1]
    R = T // CHUNKS
    S = T // n_t
    per = dn_ref.shape[0]
    rank = uq_ref.shape[1]
    qw, kw = wq_ref.shape[1], wk_ref.shape[1]
    bf16, f32, i32 = jnp.bfloat16, jnp.float32, jnp.int32

    def tensor_peer(i):
        return lax.rem(me + i, n_t)

    def same_core(i):
        return lax.rem(chip + i, n_x) * 2 + core

    def from_chip(i):
        return lax.rem(chip + n_x - i, n_x)

    loads = [
        pltpu.make_async_copy(src, dst, ws.at[k])
        for k, (src, dst) in enumerate(
            ((wq_hbm, wq_ref), (wk_hbm, wk_ref), (wv_hbm, wv_ref), (tab_hbm, tab_ref)))
    ]
    for load in loads:
        load.start()

    barrier = pltpu.get_barrier_semaphore()
    for i in range(1, n_t):
        pl.semaphore_signal(barrier, inc=1, device_id={"tensor": tensor_peer(i)})
    for i in range(1, n_r):
        pl.semaphore_signal(barrier, inc=1, device_id={"replica": lax.rem(rep + i, n_r)})
    pl.semaphore_wait(barrier, n_t - 1 + n_r - 1)

    def remote(src, dst, send, recv, **to):
        return pltpu.make_async_remote_copy(
            src_ref=src, dst_ref=dst, send_sem=send, recv_sem=recv, device_id=to)

    def rows_of(c):
        return pl.ds(pl.multiple_of(c * R, R), R)

    def meta_copy(i):
        return remote(meta_ref, meta.at[rep], ms.at[i], mr.at[i], replica=lax.rem(rep + i, n_r))

    for i in range(1, n_r):
        meta_copy(i).start()
    meta[rep] = meta_ref[...]
    for i in range(1, n_r):
        slot = lax.rem(rep + n_r - i, n_r)
        remote(meta.at[slot], meta.at[slot], ms.at[i], mr.at[i], replica=rep).wait_recv()
    own_len = meta_ref[0:1, :]
    offs = []
    total = jnp.zeros_like(own_len)
    own_off = total
    for r in range(n_r):
        offs.append(total)
        own_off = jnp.where(rep == r, total, own_off)
        total = total + meta[r, 0:1, :]

    def send_pack(c, carry):
        width = n_r * R
        g = lax.broadcasted_iota(i32, (width, B), 0)
        t = lax.broadcasted_iota(i32, (width, B), 1)
        owner = lax.rem(g // R, n_x) * 2 + g // (R * n_x)
        place = owner * T + c * R + lax.rem(g, R)
        pick = (place == t + own_off[:, 0:1]) & (t < own_len[:, 0:1])
        rows = jnp.dot(pick.astype(f32).astype(bf16), x_ref[...], preferred_element_type=f32)
        packed[c] = rows.astype(bf16).reshape(2, n_x, R, F)
        mate_copy(c).start()
        return carry

    def mate_copy(c):
        return remote(packed.at[c, 1 - core], mb.at[c], as_.at[c], ar_.at[c], replica=mate)

    def chip_copy(c, i):
        return remote(zb.at[c, lax.rem(chip + i, n_x)], xb.at[c, i], bs.at[c, i], br.at[c, i], replica=same_core(i))

    def send_chip(c, carry):
        mate_copy(c).wait_recv()
        zb[c] = packed[c, core] + mb[c]
        for i in range(1, n_x):
            chip_copy(c, i).start()
        return carry

    def pack_step(c, carry):
        send_pack(c, carry)
        send_chip(c - 1, carry)
        return carry

    send_pack(0, 0)
    lax.fori_loop(1, CHUNKS, pack_step, 0)
    send_chip(CHUNKS - 1, 0)

    pools = ((dn_ref, dg), (uq_ref, ugq), (uv_ref, ugv))

    def pool_copy(k, slot, i, j, to, own):
        src = pools[k][0] if own else pools[k][1].at[slot]
        return remote(src, pools[k][1].at[slot], asend.at[k, i, j], arecv.at[k, i, j], replica=to)

    for k in range(3):
        for i in range(1, n_x):
            pool_copy(k, rep, i, 0, same_core(i), True).start()
        pool_copy(k, rep, 0, 1, mate, True).start()
        pools[k][1][rep] = pools[k][0][...]

    def item(side, d, c):
        sgn = 1 - 2 * side
        ref = xg.at[me - sgn * d, rows_of(c)]
        return remote(ref, ref, zs.at[side, d, c], zr.at[side, d, c], tensor=me + sgn)

    def arrival(side, d, c):
        sgn = 1 - 2 * side
        ref = xg.at[me - sgn * d, rows_of(c)]
        return remote(ref, ref, zs.at[side, d - 1, c], zr.at[side, d - 1, c], tensor=me)

    def inside(t):
        return (t >= 0) & (t < n_t)

    def mac(src, c, first=False):
        rows = rows_of(c)
        x = xg[src, rows]
        feat = pl.ds(pl.multiple_of(src * F, F), F)
        lo = 0
        for w_ref in (wq_ref, wk_ref, wv_ref):
            width = w_ref.shape[1]
            term = jnp.dot(x, w_ref[feat, :], preferred_element_type=f32)
            if first:
                acc[rows, lo:lo + width] = term
            else:
                acc[rows, lo:lo + width] += term
            lo += width

    def send_own(c, carry):
        value = zb[c, chip]
        for i in range(1, n_x):
            chip_copy(c, i).wait_recv()
            value = value + xb[c, i]
        xg[me, rows_of(c)] = value
        for side in range(2):
            @pl.when(inside(me + 1 - 2 * side))
            def _():
                item(side, 0, c).start()
        mac(me, c, True)
        return carry

    for load in loads:
        load.wait()
    lax.fori_loop(0, CHUNKS, send_own, 0)

    place = lax.broadcasted_iota(i32, (T, 128), 0) + rep * T
    ids = jnp.zeros((T, 128), i32)
    pos = jnp.zeros((T, 128), i32)
    for r in range(n_r):
        mine = (place >= offs[r]) & (place < offs[r] + meta[r, 0:1, :])
        ids = jnp.where(mine, meta[r, 1:2, :], ids)
        pos = jnp.where(mine, place - offs[r], pos)
    aid[...] = ids
    pick = lax.broadcasted_iota(i32, (T, B), 1) == pos[:, 0:1]
    found = jnp.dot(pick.astype(f32).astype(bf16), tab_ref[...], preferred_element_type=f32)
    H = HEAD_SIZE
    rope[0] = found[:, 0:H] + found[:, H:2 * H] + found[:, 2 * H:3 * H]
    rope[1] = found[:, 3 * H:4 * H] + found[:, 4 * H:5 * H] + found[:, 5 * H:6 * H]

    def return_copy(slot, c, i, j, to):
        ref = qg.at[slot, rows_of(c)]
        return remote(ref, ref, es.at[c, i, j], er.at[c, i, j], replica=to)

    def finish(c):
        rows = rows_of(c)
        for lo in range(0, qw + 2 * kw, H):
            v = acc[rows, lo:lo + H]
            if lo < qw + kw:
                v = v * rope[0, rows] + pltpu.roll(v, H // 2, 1) * rope[1, rows]
            qg[rep, rows, lo:lo + H] = v.astype(bf16)
        for i in range(1, n_x):
            return_copy(rep, c, i, 0, same_core(i)).start()
        return_copy(rep, c, 0, 1, mate).start()

    def pass_on(c):
        for i in range(1, n_x):
            slot = from_chip(i) * 2 + core
            return_copy(slot, c, i, 0, rep).wait_recv()
            return_copy(slot, c, i, 1, mate).start()

    def phase(first, last, end=False):
        def step(k, carry):
            d, c = k // CHUNKS + 1, lax.rem(k, CHUNKS)

            def one(side, carry):
                sgn = 1 - 2 * side
                src = me - sgn * d

                @pl.when(inside(src))
                def _():
                    arrival(side, d, c).wait_recv()
                    if not end:
                        @pl.when(inside(me + sgn))
                        def _():
                            item(side, d, c).start()

                    mac(src, c)

                return carry

            lax.fori_loop(0, 2, one, 0)
            if end:
                finish(c)

                @pl.when(c > 0)
                def _():
                    pass_on(c - 1)

            return carry

        lax.fori_loop(first, last, step, 0)

    phase(0, (n_t - 2) * CHUNKS)

    for i in range(1, n_x):
        slot = from_chip(i) * 2 + core
        for k in range(3):
            pool_copy(k, slot, i, 0, mate, False).wait_recv()
            pool_copy(k, slot, i, 1, mate, False).start()
    for i in range(n_x):
        slot = from_chip(i) * 2 + 1 - core
        for k in range(3):
            pool_copy(k, slot, i, 1, mate, False).wait_recv()

    part[...] = jnp.zeros_like(part)

    def down(a, carry):
        term = jnp.dot(xg[me], dg[a // per, lax.rem(a, per)], preferred_element_type=f32)
        part[...] += jnp.where(aid[...] == a, term, 0.0)
        return carry

    lax.fori_loop(0, n_r * per, down, 0)

    def share(t):
        return pl.ds(pl.multiple_of(t * S, S), S)

    def rs_copy(i):
        t = tensor_peer(i)
        return remote(part.at[share(t)], pr.at[me], rs_s.at[i], rs_r.at[i], tensor=t)

    def ag_copy(i):
        return remote(sh, shg.at[share(me)], ag_s.at[i], ag_r.at[i], tensor=tensor_peer(i))

    for i in range(1, n_t):
        rs_copy(i).start()
    pr[me] = part[share(me)]

    for i in range(1, n_t):
        ref = pr.at[lax.rem(me + n_t - i, n_t)]
        remote(ref, ref, rs_s.at[i], rs_r.at[i], tensor=me).wait_recv()
    summed = pr[0]
    for t in range(1, n_t):
        summed = summed + pr[t]
    sh[...] = summed.astype(bf16)
    for i in range(1, n_t):
        ag_copy(i).start()
    shg[share(me)] = sh[...]
    for i in range(1, n_t):
        ref = shg.at[share(lax.rem(me + n_t - i, n_t))]
        remote(ref, ref, ag_s.at[i], ag_r.at[i], tensor=me).wait_recv()

    def up(a, carry):
        mine = jnp.where(aid[...] == a, shg[...].astype(f32), 0.0).astype(bf16)
        acc[:, 0:qw] += jnp.dot(mine[:, :rank], ugq[a // per, lax.rem(a, per)], preferred_element_type=f32)
        acc[:, qw + kw:] += jnp.dot(mine[:, rank:], ugv[a // per, lax.rem(a, per)], preferred_element_type=f32)
        return carry

    lax.fori_loop(0, n_r * per, up, 0)

    phase((n_t - 2) * CHUNKS, (n_t - 1) * CHUNKS, True)
    pass_on(CHUNKS - 1)

    for c in range(CHUNKS):
        for i in range(n_x):
            return_copy(from_chip(i) * 2 + 1 - core, c, i, 1, rep).wait_recv()

    tile = 256

    def unpack(k, carry):
        t = lax.broadcasted_iota(i32, (tile, T), 0) + k * tile
        g = lax.broadcasted_iota(i32, (tile, T), 1)
        rows = None
        for r in range(n_r):
            pick = (g + r * T == t + own_off[:, 0:1]) & (t < own_len[:, 0:1])
            term = jnp.dot(pick.astype(f32).astype(bf16), qg[r], preferred_element_type=f32)
            rows = term if rows is None else rows + term
        out_ref[pl.ds(pl.multiple_of(k * tile, tile), tile), :] = rows.astype(bf16)
        return carry

    lax.fori_loop(0, B // tile, unpack, 0)

    def drain(k, carry):
        d, c = k // CHUNKS, lax.rem(k, CHUNKS)
        for side in range(2):
            sgn = 1 - 2 * side

            @pl.when(inside(me - sgn * d) & inside(me + sgn))
            def _():
                item(side, d, c).wait_send()
        return carry

    lax.fori_loop(0, (n_t - 1) * CHUNKS, drain, 0)
    for i in range(1, n_t):
        rs_copy(i).wait_send()
        ag_copy(i).wait_send()
    for i in range(1, n_r):
        meta_copy(i).wait_send()
    for k in range(3):
        pool_copy(k, rep, 0, 1, mate, True).wait_send()
        for i in range(1, n_x):
            pool_copy(k, rep, i, 0, same_core(i), True).wait_send()
            pool_copy(k, from_chip(i) * 2 + core, i, 1, mate, False).wait_send()

    def drain_chunk(c, carry):
        mate_copy(c).wait_send()
        return_copy(rep, c, 0, 1, mate).wait_send()
        for i in range(1, n_x):
            chip_copy(c, i).wait_send()
            return_copy(rep, c, i, 0, same_core(i)).wait_send()
            return_copy(from_chip(i) * 2 + core, c, i, 1, mate).wait_send()
        return carry

    lax.fori_loop(0, CHUNKS, drain_chunk, 0)


def attend_kernel(qw, kw, length_ref, page_ref, qkv_ref, out_ref, pages_ref):
    T = qkv_ref.shape[0]
    tile = 256
    group = qw // kw
    length = length_ref[0]
    for p in range(T // PAGE):
        at = page_ref[0, p]
        pages_ref[at, 0] = qkv_ref[p * PAGE:(p + 1) * PAGE, qw:qw + kw]
        pages_ref[at, 1] = qkv_ref[p * PAGE:(p + 1) * PAGE, qw + kw:]
    for i in range(T // tile):
        rows = slice(i * tile, (i + 1) * tile)
        past = i * tile
        t = lax.broadcasted_iota(jnp.int32, (tile, tile), 0)
        causal = lax.broadcasted_iota(jnp.int32, (tile, tile), 1) <= t
        live = lax.broadcasted_iota(jnp.int32, (tile, HEAD_SIZE), 0) + i * tile < length
        for h in range(qw // HEAD_SIZE):
            g = (h // group) * HEAD_SIZE
            q = qkv_ref[rows, h * HEAD_SIZE:(h + 1) * HEAD_SIZE]
            pieces = [(past, past + tile, True)] + ([(0, past, False)] if past else [])
            scores = []
            for lo, hi, diagonal in pieces:
                key = qkv_ref[lo:hi, qw + g:qw + g + HEAD_SIZE]
                piece = lax.dot_general(q, key, (((1,), (1,)), ((), ())), preferred_element_type=jnp.float32)
                scores.append(jnp.where(causal, piece, -jnp.inf) if diagonal else piece)
            peak = functools.reduce(jnp.maximum, [jnp.max(p, axis=-1, keepdims=True) for p in scores])
            weights = [jnp.exp((p - peak) * HEAD_SIZE ** -0.5) for p in scores]
            inverse = 1.0 / sum(jnp.sum(w, axis=-1, keepdims=True) for w in weights)
            mixed = jnp.zeros((tile, HEAD_SIZE), jnp.float32)
            for (lo, hi, _), w in zip(pieces, weights):
                val = qkv_ref[lo:hi, qw + kw + g:qw + kw + g + HEAD_SIZE]
                mixed = mixed + jnp.dot((w * inverse).astype(jnp.bfloat16), val, preferred_element_type=jnp.float32)
            out_ref[rows, h * HEAD_SIZE:(h + 1) * HEAD_SIZE] = jnp.where(live, mixed, 0.0).astype(jnp.bfloat16)


def body(n_t, n_r, tokens, lengths, block_adapter_index, cache_page_index, query_matrix, key_matrix, value_matrix,
         down_factors, query_up_factors, value_up_factors):
    B, F = tokens.shape[1:]
    T = B // 2
    R = T // CHUNKS
    qw, kw = query_matrix.shape[1], key_matrix.shape[1]
    W = qw + 2 * kw
    rank = query_up_factors.shape[1]
    bf16, f32, i32 = jnp.bfloat16, jnp.float32, jnp.int32
    pair = jnp.concatenate([lengths, block_adapter_index, jnp.zeros((6,), i32)])
    meta = jnp.broadcast_to(pair[:, None], (8, 128))
    n_x = n_r // 2
    vmem = pl.BlockSpec(memory_space=pltpu.VMEM)
    smem = pl.BlockSpec(memory_space=pltpu.SMEM)
    dma = pltpu.SemaphoreType.DMA
    qkv = pl.pallas_call(
        functools.partial(project_kernel, n_t, n_r),
        out_shape=jax.ShapeDtypeStruct((B, W), bf16),
        in_specs=[vmem] * 2 + [pl.BlockSpec(memory_space=pl.ANY)] * 4 + [vmem] * 3,
        out_specs=vmem,
        scratch_shapes=[
            pltpu.VMEM((n_r, 8, 128), i32),
            pltpu.VMEM((CHUNKS, 2, n_x, R, F), bf16),
            pltpu.VMEM((CHUNKS, n_x, R, F), bf16),
            pltpu.VMEM((CHUNKS, n_x, R, F), bf16),
            pltpu.VMEM((CHUNKS, n_x, R, F), bf16),
            pltpu.VMEM((n_t, T, F), bf16),
            pltpu.VMEM((T, W), f32),
            pltpu.VMEM((T, 128), i32),
            pltpu.VMEM((2, T, HEAD_SIZE), f32),
            pltpu.VMEM((n_r,) + down_factors.shape, bf16),
            pltpu.VMEM((n_r,) + query_up_factors.shape, bf16),
            pltpu.VMEM((n_r,) + value_up_factors.shape, bf16),
            pltpu.VMEM((T, 2 * rank), f32),
            pltpu.VMEM((n_t, T // n_t, 2 * rank), f32),
            pltpu.VMEM((T // n_t, 2 * rank), bf16),
            pltpu.VMEM((T, 2 * rank), bf16),
            pltpu.VMEM((n_r, T, W), bf16),
            dma((n_r,)), dma((n_r,)),
            dma((CHUNKS,)), dma((CHUNKS,)),
            dma((CHUNKS, n_x)), dma((CHUNKS, n_x)),
            dma((2, n_t - 1, CHUNKS)), dma((2, n_t - 1, CHUNKS)),
            dma((3, n_x, 2)), dma((3, n_x, 2)),
            dma((n_t,)), dma((n_t,)), dma((n_t,)), dma((n_t,)),
            dma((CHUNKS, n_x, 2)), dma((CHUNKS, n_x, 2)),
            pltpu.VMEM((B, 6 * HEAD_SIZE), bf16),
            pltpu.VMEM(query_matrix.shape, bf16),
            pltpu.VMEM(key_matrix.shape, bf16),
            pltpu.VMEM(value_matrix.shape, bf16),
            dma((4,)),
        ],
        compiler_params=pltpu.CompilerParams(
            collective_id=0, has_side_effects=True, vmem_limit_bytes=58 * 1024 * 1024),
        name="project",
    )(tokens[0], meta, jnp.asarray(rope_tables(B, HEAD_SIZE)), query_matrix, key_matrix, value_matrix,
      down_factors, query_up_factors, value_up_factors)
    attended, pages = pl.pallas_call(
        functools.partial(attend_kernel, qw, kw),
        out_shape=(
            jax.ShapeDtypeStruct((B, qw), bf16),
            jax.ShapeDtypeStruct((B // PAGE, 2, PAGE, kw), bf16),
        ),
        in_specs=[smem, smem, vmem],
        out_specs=(vmem, vmem),
        compiler_params=pltpu.CompilerParams(vmem_limit_bytes=48 * 1024 * 1024),
        name="attend",
    )(lengths, cache_page_index, qkv)
    return attended[None], pages[None]


def solution(mesh):
    in_specs = (
        P(("groups", "replica"), None, "tensor"),
        P(("groups", "replica")),
        P(("groups", "replica")),
        P(("groups", "replica"), None),
        P(None, "tensor"),
        P(None, "tensor"),
        P(None, "tensor"),
        P("replica", "tensor", None),
        P("replica", None, "tensor"),
        P("replica", None, "tensor"),
    )
    out_specs = (
        P(("groups", "replica"), None, "tensor"),
        P(("groups", "replica"), None, None, None, "tensor"),
    )
    return jax.shard_map(
        functools.partial(body, mesh.shape["tensor"], mesh.shape["replica"]),
        mesh=mesh, in_specs=in_specs, out_specs=out_specs, check_vma=False)
```
